32 devices in a mesh: gx: 8 (over z, core), gy: 4 (over y, x).
Axes of the slice: x: 2, y: 2, z: 4, core: 2. Of those that a mesh axis runs over, the one named last changes fastest.
Arguments:
- obj_field: float32 [2, 2, 2048, 4096], P(None, None, 'gy', 'gx'), may hold values from -0.8 to 0.8
- probe_modes: float32 [2, 2, 256, 256], P(None, None, 'gx'), may hold values from -6 to 6
- positions: int32 [4, 8, 6, 2], P('gy', 'gx'), may hold values from 0 to 511
- counts: int32 [4, 8], P('gy', 'gx'), may hold values from 1 to 6, as said below
- amplitudes: float32 [4, 8, 6, 256, 256], P('gy', 'gx'), may hold values from 0.6 to 1.8
Outputs:
- obj_grad: float32 [2, 2, 2048, 4096], P(None, None, 'gy', 'gx')
- probe_grad: float32 [2, 2, 256, 256], P(None, None, 'gx')
The draws below stay inside these ranges and needn't reach their ends.
Inputs may be any that keep to these rules, and one draw needn't show every extreme that they name: `counts`: each tile has between 1 and 6 used slots and at least one tile uses all 6.
All inputs are finite; a program needn't handle non-finite values.
Results may differ from the reference program's by a relative error of at most 0.00014.
Values sent between devices are 32-bit elements; how exact they have to be, the bound alone decides.
A program may use at most 128 MiB of HBM per device.

```python
import math
import jax
import jax.numpy as jnp
from jax import lax

PROBE = 256
MODES = 2
SLICES = 2
BAND = 48
TILE = 512
P_MAX = 6
NROWS = 2048
NCOLS = 4096
N_GX = 8
N_GY = 4


def draw_counts(key, part):
    key = jax.random.fold_in(key, 11)
    first_key, second_key, third_key = jax.random.split(key, 3)
    baseline = jax.random.randint(first_key, (N_GY, N_GX), 1, P_MAX // 2 + 1)
    crowded = jax.random.randint(second_key, (N_GY, N_GX), 0, 8) == 0
    chosen = jax.random.randint(third_key, (), 0, N_GY * N_GX)
    picked = jnp.arange(N_GY * N_GX).reshape(N_GY, N_GX) == chosen
    return jnp.where(crowded | picked, P_MAX, baseline).astype(jnp.int32)


def place_ends(array, key, least, high):
    shape = array.shape
    index_at = [jax.random.randint(jax.random.fold_in(key, axis), (), 0, shape[axis]) for axis in range(len(shape))]
    array = array.at[tuple(index_at)].set(least)
    longest = shape.index(max(shape))
    index_at[longest] = (index_at[longest] + 1) % shape[longest]
    return array.at[tuple(index_at)].set(high)


def steps_of(rng, extent, cuts, smallest, high):
    level = 1.0
    for position, shards_of in cuts:
        heights = jax.random.uniform(jax.random.fold_in(jax.random.fold_in(rng, 6), position), (shards_of,), jnp.float32, smallest / len(cuts), high / len(cuts))
        level = level * jnp.repeat(jnp.exp(heights), extent[position] // shards_of).reshape((-1,) + (1,) * (len(extent) - 1 - position))
    return level


def gaussian(rng, shape, width, most, cuts=(), kind=jnp.bfloat16):
    gain = steps_of(rng, shape, cuts, -0.22, 0.18) if cuts else 1.0
    entries = jax.random.normal(rng, shape, jnp.float32) * width * gain
    return jnp.minimum(jnp.maximum(entries, -most), most).astype(kind)


def setup_inputs(seed: int = 0) -> dict:
    splits = jax.random.split(jax.random.key(seed), 6)
    return {
        "obj_field": jnp.clip(jax.random.uniform(splits[0], (SLICES, 2, NROWS, NCOLS), jnp.float32, -0.8, 0.8) * steps_of(splits[0], (SLICES, 2, NROWS, NCOLS), ((2, 4), (3, 8)), -0.4, 0.0), -0.8, 0.8),
        "probe_modes": gaussian(splits[1], (MODES, 2, PROBE, PROBE), 1.0, 6.0, ((2, 8),), jnp.float32),
        "positions": place_ends(jax.random.randint(splits[2], (N_GY, N_GX, P_MAX, 2), 0, TILE), jax.random.fold_in(splits[2], 1), 0, TILE - 1).astype(jnp.int32),
        "counts": draw_counts(jax.random.fold_in(splits[5], 71), 0),
        "amplitudes": jnp.clip(0.6 + 1.1999999 * jax.random.uniform(splits[4], (N_GY, N_GX, P_MAX, PROBE, PROBE), jnp.float32) ** steps_of(splits[4], (N_GY, N_GX, P_MAX, PROBE, PROBE), ((0, 4), (1, 8)), -0.2, 0.2), 0.6, 1.8),
    }


def tables_for(probe_len, ftype):
    indices = jnp.arange(probe_len, dtype=jnp.int32)
    offsets = (indices[:, None] - indices[None, :]).astype(ftype)
    chirp = math.pi * offsets * offsets / (2.0 * BAND)
    inside = jnp.where(jnp.abs(offsets) <= BAND, 1.0, 0.0).astype(ftype) / math.sqrt(2.0 * BAND + 1.0)
    cycles = (indices[:, None] * indices[None, :] % probe_len).astype(ftype)
    angles = -2.0 * math.pi * cycles / probe_len
    scaling = 1.0 / math.sqrt(probe_len)
    return (jnp.cos(chirp) * inside, jnp.sin(chirp) * inside, jnp.cos(angles) * scaling, jnp.sin(angles) * scaling)

def left_apply(mat_re, mat_im, wave_re, wave_im):
    highest = lax.Precision.HIGHEST
    out_re = jnp.einsum('ab,mbc->mac', mat_re, wave_re, precision=highest) - jnp.einsum('ab,mbc->mac', mat_im, wave_im, precision=highest)
    out_im = jnp.einsum('ab,mbc->mac', mat_re, wave_im, precision=highest) + jnp.einsum('ab,mbc->mac', mat_im, wave_re, precision=highest)
    return (out_re, out_im)

def right_apply(mat_re, mat_im, wave_re, wave_im):
    highest = lax.Precision.HIGHEST
    out_re = jnp.einsum('mab,bc->mac', wave_re, mat_re, precision=highest) - jnp.einsum('mab,bc->mac', wave_im, mat_im, precision=highest)
    out_im = jnp.einsum('mab,bc->mac', wave_im, mat_re, precision=highest) + jnp.einsum('mab,bc->mac', wave_re, mat_im, precision=highest)
    return (out_re, out_im)

def position_loss(window, mode_set, amplitude, weight, tables):
    prop_re, prop_im, four_re, four_im = tables
    wave_re = mode_set[:, 0] * window[0, 0] - mode_set[:, 1] * window[0, 1]
    wave_im = mode_set[:, 0] * window[0, 1] + mode_set[:, 1] * window[0, 0]
    for slice_index in range(1, window.shape[0]):
        wave_re, wave_im = left_apply(prop_re, prop_im, wave_re, wave_im)
        wave_re, wave_im = right_apply(prop_re, prop_im, wave_re, wave_im)
        trans_re = window[slice_index, 0]
        trans_im = window[slice_index, 1]
        wave_re, wave_im = (wave_re * trans_re - wave_im * trans_im, wave_re * trans_im + wave_im * trans_re)
    far_re, far_im = left_apply(four_re, four_im, wave_re, wave_im)
    far_re, far_im = right_apply(four_re, four_im, far_re, far_im)
    intensity = lax.optimization_barrier(jnp.sum(far_re * far_re + far_im * far_im, axis=0))
    misfit = jnp.sqrt(intensity + 1.0) - amplitude
    return weight * jnp.sum(misfit * misfit)

def reference(obj_field, probe_modes, positions, counts, amplitudes):
    ftype = obj_field.dtype
    tables = tables_for(PROBE, ftype)
    padded = jnp.pad(obj_field, ((0, 0), (0, 0), (0, PROBE), (0, PROBE)))
    per_row = N_GX * P_MAX
    anchor = jnp.int32(0)

    def visit(number, running):
        grad_pad, grad_probe = running
        number = number.astype(jnp.int32)
        row_dev = number // per_row
        col_dev = number // P_MAX % N_GX
        slot_index = number % P_MAX
        row_at = (row_dev * TILE + positions[row_dev, col_dev, slot_index, 0]).astype(jnp.int32)
        col_at = (col_dev * TILE + positions[row_dev, col_dev, slot_index, 1]).astype(jnp.int32)
        weight = jnp.where(slot_index < counts[row_dev, col_dev], 1.0, 0.0).astype(ftype)
        starts = (anchor, anchor, row_at, col_at)
        window = lax.dynamic_slice(padded, starts, (SLICES, 2, PROBE, PROBE))
        window_grad, modes_grad = jax.grad(position_loss, argnums=(0, 1))(window, probe_modes, amplitudes[row_dev, col_dev, slot_index], weight, tables)
        current = lax.dynamic_slice(grad_pad, starts, (SLICES, 2, PROBE, PROBE))
        grad_pad = lax.dynamic_update_slice(grad_pad, current + window_grad, starts)
        return (grad_pad, grad_probe + modes_grad)
    grad_pad, grad_probe = lax.fori_loop(jnp.int32(0), jnp.int32(N_GY * N_GX * P_MAX), visit, (jnp.zeros_like(padded), jnp.zeros_like(probe_modes)))
    return (grad_pad[:, :, :N_GY * TILE, :N_GX * TILE], grad_probe)
```

```python
import functools
import math

import jax
import jax.numpy as jnp
import numpy as np
from jax import lax
from jax.experimental import pallas as pl
from jax.experimental.pallas import tpu as pltpu
from jax.sharding import PartitionSpec as P

BAND = 48
LANES = 128
ROWS = 8
VMEM_BYTES = 56 * 1024 * 1024


def shifted(x, axis, by):
    length = lax.axis_size(axis)
    pairs = [(i, i + by) for i in range(length) if 0 <= i + by < length]
    return lax.ppermute(x, axis, pairs)


def real_form(mat):
    full = np.block([[mat.real, -mat.imag], [mat.imag, mat.real]])
    parts = []
    for form in (full, full.T):
        form = form.astype(np.float32)
        high = form.astype(jnp.bfloat16)
        low = (form - high.astype(np.float32)).astype(jnp.bfloat16)
        parts += [high, low]
    return np.stack(parts)


def tables_for(probe_len):
    indices = np.arange(probe_len)
    offsets = (indices[:, None] - indices[None, :]).astype(np.float64)
    prop = np.where(
        np.abs(offsets) <= BAND, np.exp(1j * math.pi * offsets * offsets / (2.0 * BAND)), 0.0
    ) / math.sqrt(2.0 * BAND + 1.0)
    cycles = (indices[:, None] * indices[None, :]) % probe_len
    four = np.exp(-2j * math.pi * cycles / probe_len) / math.sqrt(probe_len)
    return real_form(prop), real_form(four)


def split(x):
    high = x.astype(jnp.bfloat16)
    low = (x - high.astype(jnp.float32)).astype(jnp.bfloat16)
    return high, low


def dot(a, b):
    return jnp.dot(a, b, preferred_element_type=jnp.float32)


def left(table, which, x):
    high, low = split(x)
    return dot(table[which], high) + dot(table[which], low) + dot(table[which + 1], high)


def right(x, table, which):
    high, low = split(x)
    return dot(high, table[which]) + dot(low, table[which]) + dot(high, table[which + 1])


def blocks(x):
    h = x.shape[0] // 2
    return x[:h, :h], x[:h, h:], x[h:, :h], x[h:, h:]


def joined(a, b, c, d):
    return jnp.concatenate(
        [jnp.concatenate([a, b], axis=1), jnp.concatenate([c, d], axis=1)], axis=0
    )


def swapped(x):
    a, b, c, d = blocks(x)
    return joined(a, c, b, d)


def window_of(ext, plane, row, col, size):
    base = pl.multiple_of(col // LANES * LANES, LANES)
    top = pl.multiple_of(row // ROWS * ROWS, ROWS)
    off, down = col - base, row - top
    wide = ext[plane, pl.ds(top, size + ROWS), pl.ds(base, size + LANES)]
    tall = wide.reshape(size // ROWS + 1, ROWS, size + LANES)
    tall = pltpu.roll(tall, lax.rem(ROWS - down, ROWS), 1)
    keep = lax.broadcasted_iota(jnp.int32, (1, ROWS, size + LANES), 1) < ROWS - down
    wide = jnp.where(keep, tall[:-1], tall[1:]).reshape(size, size + LANES)
    count = size // LANES
    turn = lax.rem(LANES - off, LANES)
    turned = [
        pltpu.roll(wide[:, k * LANES : (k + 1) * LANES], turn, 1) for k in range(count + 1)
    ]
    keep = lax.broadcasted_iota(jnp.int32, (size, LANES), 1) < LANES - off
    return jnp.concatenate(
        [jnp.where(keep, turned[k], turned[k + 1]) for k in range(count)], axis=1
    )


def add_window(ext, plane, row, col, grad):
    size = grad.shape[0]
    base = pl.multiple_of(col // LANES * LANES, LANES)
    top = pl.multiple_of(row // ROWS * ROWS, ROWS)
    off, down = col - base, row - top
    count = size // LANES
    turned = [pltpu.roll(grad[:, k * LANES : (k + 1) * LANES], off, 1) for k in range(count)]
    keep = lax.broadcasted_iota(jnp.int32, (size, LANES), 1) >= off
    zero = jnp.zeros((size, LANES), jnp.float32)
    turned = [zero] + turned + [zero]
    wide = jnp.concatenate(
        [jnp.where(keep, turned[k + 1], turned[k]) for k in range(count + 1)], axis=1
    )
    tall = pltpu.roll(wide.reshape(size // ROWS, ROWS, size + LANES), down, 1)
    keep = lax.broadcasted_iota(jnp.int32, (1, ROWS, size + LANES), 1) >= down
    zero = jnp.zeros((1, ROWS, size + LANES), jnp.float32)
    above = jnp.concatenate([zero, tall], axis=0)
    here = jnp.concatenate([tall, zero], axis=0)
    wide = jnp.where(keep, here, above).reshape(size + ROWS, size + LANES)
    ext[plane, pl.ds(top, size + ROWS), pl.ds(base, size + LANES)] += wide


def regions(ext, tile, size):
    return (
        ext.at[:, pl.ds(0, tile), pl.ds(0, tile)],
        ext.at[:, pl.ds(0, tile), pl.ds(tile, size)],
        ext.at[:, pl.ds(tile, size), pl.ds(0, tile)],
        ext.at[:, pl.ds(tile, size), pl.ds(tile, size)],
    )


def fetch(pieces, ext, sems, tile, size):
    copies = [
        pltpu.make_async_copy(piece, region, sems.at[k])
        for k, (piece, region) in enumerate(zip(pieces, regions(ext, tile, size)))
    ]
    for copy in copies:
        copy.start()
    for copy in copies:
        copy.wait()


def flush(ext, pieces, sems, tile, size):
    copies = [
        pltpu.make_async_copy(region, piece, sems.at[k])
        for k, (piece, region) in enumerate(zip(pieces, regions(ext, tile, size)))
    ]
    for copy in copies:
        copy.start()
    for copy in copies:
        copy.wait()


def forward_kernel(tile, size, cnt, pos, own, rgt, low, cor, probe, table, out, ext, sems):
    j = pl.program_id(0)

    @pl.when(j == 0)
    def _():
        fetch((own, rgt, low, cor), ext, sems, tile, size)

    @pl.when(j < cnt[0])
    def _():
        row, col = pos[2 * j], pos[2 * j + 1]
        wr = window_of(ext, 0, row, col, size)
        wi = window_of(ext, 1, row, col, size)
        waves = []
        for m in range(2):
            pr, pi = probe[m, 0], probe[m, 1]
            waves += [pr * wr - pi * wi, pr * wi + pi * wr]
        x = right(joined(*waves), table, 2)
        out[0] = left(table, 0, swapped(x))


def middle_kernel(
    tile, size, cnt, pos, own, rgt, low, cor, wave, amp, table,
    gwave, g_own, g_rgt, g_low, g_cor, ext, gext, sems,
):
    j = pl.program_id(0)

    @pl.when(j == 0)
    def _():
        fetch((own, rgt, low, cor), ext, sems, tile, size)
        gext[...] = jnp.zeros_like(gext)

    @pl.when(j < cnt[0])
    def _():
        row, col = pos[2 * j], pos[2 * j + 1]
        wr = window_of(ext, 0, row, col, size)
        wi = window_of(ext, 1, row, col, size)
        u0r, u1r, u0i, u1i = blocks(wave[0])
        x = joined(
            u0r * wr - u0i * wi, u1r * wr - u1i * wi, u0r * wi + u0i * wr, u1r * wi + u1i * wr
        )
        x = right(swapped(left(table, 0, x)), table, 2)
        p0r, p0i, p1r, p1i = blocks(x)
        intensity = p0r * p0r + p0i * p0i + p1r * p1r + p1i * p1i
        scale = 2.0 - 2.0 * amp[0] * lax.rsqrt(intensity + 1.0)
        g = joined(p0r * scale, p0i * scale, p1r * scale, p1i * scale)
        g = left(table, 2, swapped(right(g, table, 0)))
        g0r, g1r, g0i, g1i = blocks(g)
        u0r, u1r, u0i, u1i = blocks(wave[0])
        add_window(gext, 0, row, col, u0r * g0r + u0i * g0i + u1r * g1r + u1i * g1i)
        add_window(gext, 1, row, col, u0r * g0i - u0i * g0r + u1r * g1i - u1i * g1r)
        wr = window_of(ext, 0, row, col, size)
        wi = window_of(ext, 1, row, col, size)
        gwave[0] = joined(
            wr * g0r + wi * g0i, wr * g1r + wi * g1i, wr * g0i - wi * g0r, wr * g1i - wi * g1r
        )

    @pl.when(j == pl.num_programs(0) - 1)
    def _():
        flush(gext, (g_own, g_rgt, g_low, g_cor), sems, tile, size)


def backward_kernel(
    tile, size, cnt, pos, own, rgt, low, cor, gwave, probe, table,
    g_probe, g_own, g_rgt, g_low, g_cor, ext, gext, sems,
):
    j = pl.program_id(0)

    @pl.when(j == 0)
    def _():
        fetch((own, rgt, low, cor), ext, sems, tile, size)
        gext[...] = jnp.zeros_like(gext)
        g_probe[...] = jnp.zeros_like(g_probe)

    @pl.when(j < cnt[0])
    def _():
        row, col = pos[2 * j], pos[2 * j + 1]
        g = left(table, 2, gwave[0])
        g = right(swapped(g), table, 0)
        parts = blocks(g)
        wr = window_of(ext, 0, row, col, size)
        wi = window_of(ext, 1, row, col, size)
        sum_r, sum_i = 0.0, 0.0
        for m in range(2):
            gr, gi = parts[2 * m], parts[2 * m + 1]
            pr, pi = probe[m, 0], probe[m, 1]
            sum_r += pr * gr + pi * gi
            sum_i += pr * gi - pi * gr
            g_probe[m, 0] += wr * gr + wi * gi
            g_probe[m, 1] += wr * gi - wi * gr
        add_window(gext, 0, row, col, sum_r)
        add_window(gext, 1, row, col, sum_i)

    @pl.when(j == pl.num_programs(0) - 1)
    def _():
        flush(gext, (g_own, g_rgt, g_low, g_cor), sems, tile, size)


def on_device(obj_field, probe_modes, positions, counts, amplitudes):
    modes, _, _, size = probe_modes.shape
    tile = obj_field.shape[2]
    slots = amplitudes.shape[2]
    span = tile + size
    both = 2 * size
    prop, four = tables_for(size)
    cnt = counts.reshape(1)
    pos = positions.reshape(2 * slots)
    amp = amplitudes.reshape(slots, size, size)
    probe = lax.all_gather(probe_modes, "gx", axis=2, tiled=True)

    def halo(part):
        lower = shifted(part[:, :size, :], "gy", -1)
        rightward = shifted(part[:, :, :size], "gx", -1)
        corner = shifted(lower[:, :, :size], "gx", -1)
        return part, rightward, lower, corner

    first = halo(obj_field[0])
    after, _ = lax.optimization_barrier((obj_field[1], first[2]))
    second = halo(after)

    anywhere = pl.BlockSpec(memory_space=pl.ANY)
    per_slot = lambda *shape: pl.BlockSpec(
        (1,) + shape, lambda j, c, p: (jnp.minimum(j, c[0] - 1),) + (0,) * len(shape)
    )
    whole = lambda *shape: pl.BlockSpec(shape, lambda j, c, p: (0,) * len(shape))
    f32 = lambda *shape: jax.ShapeDtypeStruct(shape, jnp.float32)
    piece_shapes = (
        f32(2, tile, tile), f32(2, tile, size), f32(2, size, tile), f32(2, size, size)
    )
    ext = pltpu.VMEM((2, span, span), jnp.float32)
    sems = pltpu.SemaphoreType.DMA((4,))
    params = pltpu.CompilerParams(vmem_limit_bytes=VMEM_BYTES)
    wave_spec = per_slot(both, both)
    table_spec = whole(4, both, both)
    probe_spec = whole(modes, 2, size, size)
    work = 3 * 2 * 2 * both**3 * slots

    def call(kernel, in_specs, out_specs, out_shape, scratch, flops):
        return pl.pallas_call(
            functools.partial(kernel, tile, size),
            grid_spec=pltpu.PrefetchScalarGridSpec(
                num_scalar_prefetch=2,
                grid=(slots,),
                in_specs=in_specs,
                out_specs=out_specs,
                scratch_shapes=scratch,
            ),
            out_shape=out_shape,
            compiler_params=params,
            cost_estimate=pl.CostEstimate(
                flops=flops, bytes_accessed=16 * 1024 * 1024, transcendentals=0
            ),
        )

    wave = call(
        forward_kernel,
        [anywhere] * 4 + [probe_spec, table_spec],
        wave_spec,
        f32(slots, both, both),
        [ext, sems],
        work,
    )(cnt, pos, *first, probe, prop)
    gwave, *grads_1 = call(
        middle_kernel,
        [anywhere] * 4 + [wave_spec, per_slot(size, size), table_spec],
        [wave_spec] + [anywhere] * 4,
        (f32(slots, both, both),) + piece_shapes,
        [ext, ext, sems],
        2 * work,
    )(cnt, pos, *second, wave, amp, four)
    g_probe, *grads_0 = call(
        backward_kernel,
        [anywhere] * 4 + [wave_spec, probe_spec, table_spec],
        [probe_spec] + [anywhere] * 4,
        (f32(modes, 2, size, size),) + piece_shapes,
        [ext, ext, sems],
        work,
    )(cnt, pos, *first, gwave, probe, prop)

    def back(grads):
        own, rightward, lower, corner = grads
        corner = shifted(corner, "gx", 1)
        rightward = shifted(rightward, "gx", 1)
        lower = shifted(lower.at[:, :, :size].add(corner), "gy", 1)
        own = own.at[:, :, :size].add(rightward)
        return own.at[:, :size, :].add(lower)

    obj_grad = jnp.stack([back(grads_0), back(grads_1)])
    rows = lax.psum_scatter(g_probe, "gx", scatter_dimension=2, tiled=True)
    probe_grad = lax.psum(rows, "gy")
    return (obj_grad, probe_grad)


def solution(mesh):
    return jax.shard_map(
        on_device,
        mesh=mesh,
        in_specs=(
            P(None, None, "gy", "gx"),
            P(None, None, "gx", None),
            P("gy", "gx", None, None),
            P("gy", "gx"),
            P("gy", "gx", None, None, None),
        ),
        out_specs=(P(None, None, "gy", "gx"), P(None, None, "gx", None)),
        check_vma=False,
    )
```

```python
import functools
import math

import jax
import jax.numpy as jnp
import numpy as np
from jax import lax
from jax.experimental import pallas as pl
from jax.experimental.pallas import tpu as pltpu
from jax.sharding import PartitionSpec as P

BAND = 48
LANES = 128
ROWS = 8
VMEM_BYTES = 56 * 1024 * 1024


def shifted(x, axis, by):
    length = lax.axis_size(axis)
    pairs = [(i, i + by) for i in range(length) if 0 <= i + by < length]
    return lax.ppermute(x, axis, pairs)


def real_form(mat):
    full = np.block([[mat.real, -mat.imag], [mat.imag, mat.real]])
    parts = []
    for form in (full, full.T):
        form = form.astype(np.float32)
        high = form.astype(jnp.bfloat16)
        low = (form - high.astype(np.float32)).astype(jnp.bfloat16)
        parts += [high, low]
    return np.stack(parts)


def tables_for(probe_len):
    indices = np.arange(probe_len)
    offsets = (indices[:, None] - indices[None, :]).astype(np.float64)
    prop = np.where(
        np.abs(offsets) <= BAND, np.exp(1j * math.pi * offsets * offsets / (2.0 * BAND)), 0.0
    ) / math.sqrt(2.0 * BAND + 1.0)
    cycles = (indices[:, None] * indices[None, :]) % probe_len
    four = np.exp(-2j * math.pi * cycles / probe_len) / math.sqrt(probe_len)
    return real_form(prop), real_form(four)


def split(x):
    high = x.astype(jnp.bfloat16)
    low = (x - high.astype(jnp.float32)).astype(jnp.bfloat16)
    return high, low


def dot(a, b):
    return jnp.dot(a, b, preferred_element_type=jnp.float32)


def left(table, which, x):
    high, low = split(x)
    return dot(table[which], high) + dot(table[which], low) + dot(table[which + 1], high)


def right(x, table, which):
    high, low = split(x)
    return dot(high, table[which]) + dot(low, table[which]) + dot(high, table[which + 1])


def blocks(x):
    h = x.shape[0] // 2
    return x[:h, :h], x[:h, h:], x[h:, :h], x[h:, h:]


def joined(a, b, c, d):
    return jnp.concatenate(
        [jnp.concatenate([a, b], axis=1), jnp.concatenate([c, d], axis=1)], axis=0
    )


def swapped(x):
    a, b, c, d = blocks(x)
    return joined(a, c, b, d)


def window_of(ext, plane, row, col, size):
    base = pl.multiple_of(col // LANES * LANES, LANES)
    top = pl.multiple_of(row // ROWS * ROWS, ROWS)
    off, down = col - base, row - top
    wide = ext[plane, pl.ds(top, size + ROWS), pl.ds(base, size + LANES)]
    tall = wide.reshape(size // ROWS + 1, ROWS, size + LANES)
    tall = pltpu.roll(tall, lax.rem(ROWS - down, ROWS), 1)
    keep = lax.broadcasted_iota(jnp.int32, (1, ROWS, size + LANES), 1) < ROWS - down
    wide = jnp.where(keep, tall[:-1], tall[1:]).reshape(size, size + LANES)
    count = size // LANES
    turn = lax.rem(LANES - off, LANES)
    turned = [
        pltpu.roll(wide[:, k * LANES : (k + 1) * LANES], turn, 1) for k in range(count + 1)
    ]
    keep = lax.broadcasted_iota(jnp.int32, (size, LANES), 1) < LANES - off
    return jnp.concatenate(
        [jnp.where(keep, turned[k], turned[k + 1]) for k in range(count)], axis=1
    )


def add_window(ext, plane, row, col, grad):
    size = grad.shape[0]
    base = pl.multiple_of(col // LANES * LANES, LANES)
    top = pl.multiple_of(row // ROWS * ROWS, ROWS)
    off, down = col - base, row - top
    count = size // LANES
    turned = [pltpu.roll(grad[:, k * LANES : (k + 1) * LANES], off, 1) for k in range(count)]
    keep = lax.broadcasted_iota(jnp.int32, (size, LANES), 1) >= off
    zero = jnp.zeros((size, LANES), jnp.float32)
    turned = [zero] + turned + [zero]
    wide = jnp.concatenate(
        [jnp.where(keep, turned[k + 1], turned[k]) for k in range(count + 1)], axis=1
    )
    tall = pltpu.roll(wide.reshape(size // ROWS, ROWS, size + LANES), down, 1)
    keep = lax.broadcasted_iota(jnp.int32, (1, ROWS, size + LANES), 1) >= down
    zero = jnp.zeros((1, ROWS, size + LANES), jnp.float32)
    above = jnp.concatenate([zero, tall], axis=0)
    here = jnp.concatenate([tall, zero], axis=0)
    wide = jnp.where(keep, here, above).reshape(size + ROWS, size + LANES)
    ext[plane, pl.ds(top, size + ROWS), pl.ds(base, size + LANES)] += wide


def regions(ext, count, tile, size):
    whole = [
        ext.at[:, pl.ds(0, tile), pl.ds(0, tile)],
        ext.at[:, pl.ds(0, tile), pl.ds(tile, size)],
    ]
    if count == 3:
        return whole + [ext.at[:, pl.ds(tile, size), :]]
    return whole + [
        ext.at[:, pl.ds(tile, size), pl.ds(0, tile)],
        ext.at[:, pl.ds(tile, size), pl.ds(tile, size)],
    ]


def run_copies(sources, targets, sems):
    copies = [
        pltpu.make_async_copy(source, target, sems.at[k])
        for k, (source, target) in enumerate(zip(sources, targets))
    ]
    for copy in copies:
        copy.start()
    for copy in copies:
        copy.wait()


def fetch(pieces, ext, sems, tile, size):
    run_copies(pieces, regions(ext, len(pieces), tile, size), sems)


def flush(ext, pieces, sems, tile, size):
    run_copies(regions(ext, len(pieces), tile, size), pieces, sems)


def forward_kernel(tile, size, cnt, pos, obj, rgt, low, cor, probe, table, out, ext, sems):
    j = pl.program_id(0)

    @pl.when(j == 0)
    def _():
        fetch((obj.at[0], rgt, low, cor), ext, sems, tile, size)

    @pl.when(j < cnt[0])
    def _():
        row, col = pos[2 * j], pos[2 * j + 1]
        wr = window_of(ext, 0, row, col, size)
        wi = window_of(ext, 1, row, col, size)
        waves = []
        for m in range(2):
            pr, pi = probe[m, 0], probe[m, 1]
            waves += [pr * wr - pi * wi, pr * wi + pi * wr]
        x = right(joined(*waves), table, 2)
        out[0] = left(table, 0, swapped(x))


def middle_kernel(
    tile, size, cnt, pos, obj, rgt, bot, wave, amp, table,
    gwave, g_obj, g_rgt, g_bot, ext, gext, sems,
):
    j = pl.program_id(0)

    @pl.when(j == 0)
    def _():
        fetch((obj.at[1], rgt, bot), ext, sems, tile, size)
        gext[...] = jnp.zeros_like(gext)

    @pl.when(j < cnt[0])
    def _():
        row, col = pos[2 * j], pos[2 * j + 1]
        wr = window_of(ext, 0, row, col, size)
        wi = window_of(ext, 1, row, col, size)
        u0r, u1r, u0i, u1i = blocks(wave[0])
        x = joined(
            u0r * wr - u0i * wi, u1r * wr - u1i * wi, u0r * wi + u0i * wr, u1r * wi + u1i * wr
        )
        x = right(swapped(left(table, 0, x)), table, 2)
        p0r, p0i, p1r, p1i = blocks(x)
        intensity = p0r * p0r + p0i * p0i + p1r * p1r + p1i * p1i
        scale = 2.0 - 2.0 * amp[0] * lax.rsqrt(intensity + 1.0)
        g = joined(p0r * scale, p0i * scale, p1r * scale, p1i * scale)
        g = left(table, 2, swapped(right(g, table, 0)))
        g0r, g1r, g0i, g1i = blocks(g)
        u0r, u1r, u0i, u1i = blocks(wave[0])
        add_window(gext, 0, row, col, u0r * g0r + u0i * g0i + u1r * g1r + u1i * g1i)
        add_window(gext, 1, row, col, u0r * g0i - u0i * g0r + u1r * g1i - u1i * g1r)
        wr = window_of(ext, 0, row, col, size)
        wi = window_of(ext, 1, row, col, size)
        gwave[0] = joined(
            wr * g0r + wi * g0i, wr * g1r + wi * g1i, wr * g0i - wi * g0r, wr * g1i - wi * g1r
        )

    @pl.when(j == pl.num_programs(0) - 1)
    def _():
        flush(gext, (g_obj.at[1], g_rgt, g_bot), sems, tile, size)


def backward_kernel(
    tile, size, cnt, pos, obj, rgt, low, cor, gwave, probe, table, _,
    g_probe, g_obj, g_rgt, g_low, g_cor, ext, gext, sems,
):
    j = pl.program_id(0)

    @pl.when(j == 0)
    def _():
        fetch((obj.at[0], rgt, low, cor), ext, sems, tile, size)
        gext[...] = jnp.zeros_like(gext)
        g_probe[...] = jnp.zeros_like(g_probe)

    @pl.when(j < cnt[0])
    def _():
        row, col = pos[2 * j], pos[2 * j + 1]
        g = left(table, 2, gwave[0])
        g = right(swapped(g), table, 0)
        parts = blocks(g)
        wr = window_of(ext, 0, row, col, size)
        wi = window_of(ext, 1, row, col, size)
        sum_r, sum_i = 0.0, 0.0
        for m in range(2):
            gr, gi = parts[2 * m], parts[2 * m + 1]
            pr, pi = probe[m, 0], probe[m, 1]
            sum_r += pr * gr + pi * gi
            sum_i += pr * gi - pi * gr
            g_probe[m, 0] += wr * gr + wi * gi
            g_probe[m, 1] += wr * gi - wi * gr
        add_window(gext, 0, row, col, sum_r)
        add_window(gext, 1, row, col, sum_i)

    @pl.when(j == pl.num_programs(0) - 1)
    def _():
        flush(gext, (g_obj.at[0], g_rgt, g_low, g_cor), sems, tile, size)


def partners(axis, bit):
    return [(i, i ^ (1 << bit)) for i in range(lax.axis_size(axis))]


def scattered_rows(x, axis):
    n = lax.axis_size(axis)
    if n & (n - 1):
        return lax.psum_scatter(x, axis, scatter_dimension=2, tiled=True)
    bits = n.bit_length() - 1
    me = lax.axis_index(axis)
    x = x.reshape(x.shape[:2] + (2,) * bits + (x.shape[2] // n, x.shape[3]))
    for bit in range(bits):
        dim = 2 + bits - 1 - bit
        mine = (me >> bit) & 1
        kept = lax.dynamic_index_in_dim(x, mine, dim, keepdims=False)
        sent = lax.dynamic_index_in_dim(x, 1 - mine, dim, keepdims=False)
        x = kept + lax.ppermute(sent, axis, partners(axis, bit))
    return x


def summed(x, axis):
    n = lax.axis_size(axis)
    if n & (n - 1):
        return lax.psum(x, axis)
    for bit in range(n.bit_length() - 1):
        x = x + lax.ppermute(x, axis, partners(axis, bit))
    return x


def on_device(obj_field, probe_modes, positions, counts, amplitudes):
    modes, _, _, size = probe_modes.shape
    tile = obj_field.shape[2]
    slots = amplitudes.shape[2]
    span = tile + size
    both = 2 * size
    prop, four = tables_for(size)
    cnt = counts.reshape(1)
    pos = positions.reshape(2 * slots)
    amp = amplitudes.reshape(slots, size, size)
    probe = lax.all_gather(probe_modes, "gx", axis=2, tiled=True)

    lower = shifted(obj_field[0, :, :size, :], "gy", -1)
    rightward = shifted(obj_field[0, :, :, :size], "gx", -1)
    right_1 = shifted(obj_field[1, :, :, :size], "gx", -1)
    corner = shifted(lower[:, :, :size], "gx", -1)
    bottom = jnp.concatenate([obj_field[1, :, :size, :], right_1[:, :size, :]], axis=2)
    bottom, lower = lax.optimization_barrier((bottom, lower))
    bottom = shifted(bottom, "gy", -1)

    anywhere = pl.BlockSpec(memory_space=pl.ANY)
    per_slot = lambda *shape: pl.BlockSpec(
        (1,) + shape, lambda j, c, p: (jnp.minimum(j, c[0] - 1),) + (0,) * len(shape)
    )
    whole = lambda *shape: pl.BlockSpec(shape, lambda j, c, p: (0,) * len(shape))
    f32 = lambda *shape: jax.ShapeDtypeStruct(shape, jnp.float32)
    obj_shape = f32(*obj_field.shape)
    right_shape = f32(2, tile, size)
    ext = pltpu.VMEM((2, span, span), jnp.float32)
    sems = pltpu.SemaphoreType.DMA((4,))
    params = pltpu.CompilerParams(vmem_limit_bytes=VMEM_BYTES)
    wave_spec = per_slot(both, both)
    table_spec = whole(4, both, both)
    probe_spec = whole(modes, 2, size, size)
    work = 3 * 2 * 2 * both**3 * slots

    def call(kernel, in_specs, out_specs, out_shape, scratch, flops, aliases):
        return pl.pallas_call(
            functools.partial(kernel, tile, size),
            grid_spec=pltpu.PrefetchScalarGridSpec(
                num_scalar_prefetch=2,
                grid=(slots,),
                in_specs=in_specs,
                out_specs=out_specs,
                scratch_shapes=scratch,
            ),
            out_shape=out_shape,
            input_output_aliases=aliases,
            compiler_params=params,
            cost_estimate=pl.CostEstimate(
                flops=flops, bytes_accessed=16 * 1024 * 1024, transcendentals=0
            ),
        )

    wave = call(
        forward_kernel,
        [anywhere] * 4 + [probe_spec, table_spec],
        wave_spec,
        f32(slots, both, both),
        [ext, sems],
        work,
        {},
    )(cnt, pos, obj_field, rightward, lower, corner, probe, prop)
    gwave, g_obj, g_right_1, g_bottom = call(
        middle_kernel,
        [anywhere] * 3 + [wave_spec, per_slot(size, size), table_spec],
        [wave_spec] + [anywhere] * 3,
        (f32(slots, both, both), obj_shape, right_shape, f32(2, size, span)),
        [ext, ext, sems],
        2 * work,
        {},
    )(cnt, pos, obj_field, right_1, bottom, wave, amp, four)
    g_bottom = shifted(g_bottom, "gy", 1)
    g_right_1 = shifted(g_right_1, "gx", 1)
    g_probe, g_obj, g_right, g_lower, g_corner = call(
        backward_kernel,
        [anywhere] * 4 + [wave_spec, probe_spec, table_spec, anywhere],
        [probe_spec] + [anywhere] * 4,
        (f32(modes, 2, size, size), obj_shape, right_shape, f32(2, size, tile), f32(2, size, size)),
        [ext, ext, sems],
        work,
        {9: 1},
    )(cnt, pos, obj_field, rightward, lower, corner, gwave, probe, prop, g_obj)

    g_corner = shifted(g_corner, "gx", 1)
    g_lower = shifted(g_lower.at[:, :, :size].add(g_corner), "gy", 1)
    g_right = shifted(g_right, "gx", 1)
    g_corner_1 = shifted(g_bottom[:, :, tile:], "gx", 1)
    probe_grad = summed(scattered_rows(g_probe, "gx"), "gy")
    g_obj = g_obj.at[1, :, :, :size].add(g_right_1)
    g_obj = g_obj.at[1, :, :size, :].add(g_bottom[:, :, :tile])
    g_obj = g_obj.at[0, :, :, :size].add(g_right)
    g_obj = g_obj.at[1, :, :size, :size].add(g_corner_1)
    g_obj = g_obj.at[0, :, :size, :].add(g_lower)
    return (g_obj, probe_grad)


def solution(mesh):
    return jax.shard_map(
        on_device,
        mesh=mesh,
        in_specs=(
            P(None, None, "gy", "gx"),
            P(None, None, "gx", None),
            P("gy", "gx", None, None),
            P("gy", "gx"),
            P("gy", "gx", None, None, None),
        ),
        out_specs=(P(None, None, "gy", "gx"), P(None, None, "gx", None)),
        check_vma=False,
    )
```
